32 devices in a mesh: groups: 2 (over x), tok: 16 (over z, y, core).
Axes of the slice: x: 2, y: 2, z: 4, core: 2. Of those that a mesh axis runs over, the one named last changes fastest.
Arguments:
- single: bfloat16 [512, 8, 768], P(('groups', 'tok')), parts along dimension 0, may hold values from -6 to 6
- pair: bfloat16 [512, 256, 128], P(('groups', 'tok')), parts along dimension 0, may hold values from -400 to 400, as said below
- chain: int32 [512], P(('groups', 'tok')), parts along dimension 0, may hold values from 0 to 7, never falling along the last dimension, each value on 1 to 64 neighbouring positions
- residue: int32 [512], P(('groups', 'tok')), parts along dimension 0, may hold values from 0 to 510, as said below
- valid: int32 [512], P(('groups', 'tok')), parts along dimension 0, may hold values 0 or 1
- w_query: bfloat16 [768, 768], replicated, may hold values from -0.21875 to 0.21875
- w_key: bfloat16 [768, 768], replicated, may hold values from -0.21875 to 0.21875
- w_value: bfloat16 [768, 768], replicated, may hold values from -0.21875 to 0.21875
- w_gate: bfloat16 [768, 768], replicated, may hold values from -0.21875 to 0.21875
- w_out: bfloat16 [768, 768], replicated, may hold values from -0.21875 to 0.21875
- w_pair: bfloat16 [128, 16], replicated, may hold values from -1.1953125 to 1.1953125
- rel_table: float32 [66, 16], replicated, may hold values from -6 to 6
Outputs:
- updated: bfloat16 [512, 8, 768], P(('groups', 'tok')), parts along dimension 0
The draws below stay inside these ranges and needn't reach their ends.
There are 2 independent parts, one for each index of `groups`. The reference program is written for one: setup_inputs(seed, part) draws one part's arguments, and reference() takes and returns one part's arrays. A program takes and returns all parts, laid end to end along the dimension named above; an argument that names none is the same for every part. Nothing has to cross between parts.
Inputs may be any that keep to these rules, and one draw needn't show every extreme that they name: `pair`: pair entries are of order one, except possibly in a few query rows where two entries have many times the usual size. `residue`: starts at 0 and rises from each token to the next, by 1 or 2 except into the last token, which holds the largest value.
All inputs are finite; a program needn't handle non-finite values. No bound on the sum of `valid` on one device may be relied on, other than what follows from the above.
Results may differ from the reference program's by a relative error of at most 0.0045.
Values may be sent and summed in bfloat16 or wider, within the bound.
A program may use at most 128 MiB of HBM per device.

```python
import math
import jax
import jax.numpy as jnp
import numpy as np
from jax import lax

D = 768
HEADS = 16
PAIR_C = 128
SAMPLES = 8
CHAINS = 8
RELBINS = 66
TOKENS = 256


def draw_pair(key, part):
    key_base = jax.random.fold_in(key, 0)
    base = jax.random.normal(key_base, (TOKENS, TOKENS, PAIR_C), jnp.float32)
    return jnp.clip(base, -400.0, 400.0).astype(jnp.bfloat16)


def draw_residue(key, part):
    steps_up = jax.random.randint(key, (TOKENS,), 1, 3)
    rising = (jnp.cumsum(steps_up) - steps_up[0]).astype(jnp.int32)
    positions = jnp.arange(TOKENS, dtype=jnp.int32)
    return jnp.where(positions == TOKENS - 1, 2 * TOKENS - 2, rising).astype(jnp.int32)


def with_ends(values, stream_key, low, top_value):
    longest = values.shape.index(max(values.shape))
    spots = []
    for shift in (0, 1):
        where = [jax.random.randint(jax.random.fold_in(stream_key, axis), (), 0, length) for axis, length in enumerate(values.shape)]
        where[longest] = (where[longest] + shift) % values.shape[longest]
        spots.append(tuple(where))
    return values.at[spots[0]].set(low).at[spots[1]].set(top_value)


def levels(stream_key, shape, cuts, low, largest):
    level = 1.0
    for dim, blocks in cuts:
        steps = jax.random.uniform(jax.random.fold_in(jax.random.fold_in(stream_key, 6), dim), (blocks,), jnp.float32, low / len(cuts), largest / len(cuts))
        level = level * jnp.repeat(jnp.exp(steps), shape[dim] // blocks).reshape((-1,) + (1,) * (len(shape) - 1 - dim))
    return level


def profile(amount, total, limit, slope):
    weights = [(1 << 20) // math.isqrt(rank ** slope) + 1 for rank in range(2, amount + 1)]
    surplus, given = total - limit - (amount - 1), [1] * (amount - 1)
    while surplus > 0:
        movable = [i for i in range(amount - 1) if given[i] < limit]
        whole, left = sum([weights[i] for i in movable]), surplus
        for i in movable:
            more = min(limit - given[i], max(1, left * weights[i] // whole), surplus)
            given[i] = given[i] + more
            surplus = surplus - more
    return np.array([limit] + given)


def ragged(stream_key, amount, total, bound, lean):
    if amount == 2:
        one = jax.random.randint(stream_key, (), max(1, total - bound), min(bound, total - 1) + 1)
        return jnp.stack([one, total - one])
    sizes = jnp.asarray(profile(amount, total, bound, lean), jnp.int32)
    pairs = (amount - 1) // 2
    donor, receiver = sizes[1:1 + 2 * pairs:2], sizes[2:2 + 2 * pairs:2]
    margin = jnp.minimum(donor - 1, bound - receiver)
    moved = jax.random.randint(jax.random.fold_in(stream_key, 1), (pairs,), 0, 1 << 20) % (margin + 1)
    sizes = sizes.at[1:1 + 2 * pairs:2].set(donor - moved).at[2:2 + 2 * pairs:2].set(receiver + moved)
    return sizes[jax.random.permutation(jax.random.fold_in(stream_key, 2), amount)]


def noise(own_key, shape, scale, reach, shards=(), kind=jnp.bfloat16):
    drawn = scale * jax.random.normal(own_key, shape, jnp.float32)
    if shards:
        drawn = drawn * levels(own_key, shape, shards, -0.22, 0.18)
    return jnp.clip(drawn, -reach, reach).astype(kind)


def setup_inputs(seed: int = 0, part: int = 0) -> dict:
    key_of = jax.random.split(jax.random.key(seed), 13)
    part_splits = jax.random.split(jax.random.fold_in(key_of[12], part), 13)
    single = noise(part_splits[0], (TOKENS, SAMPLES, D), 1.0, 6.0, ((0, 16),))
    pair = draw_pair(jax.random.fold_in(jax.random.fold_in(key_of[12], part), 71), part)
    chain = jnp.searchsorted(jnp.cumsum(ragged(part_splits[2], CHAINS, TOKENS, TOKENS // 4, 0)), jnp.arange(TOKENS), side="right").astype(jnp.int32)
    residue = draw_residue(jax.random.fold_in(jax.random.fold_in(key_of[12], part), 71), part)
    valid = with_ends((jax.random.randint(part_splits[4], (TOKENS,), 0, 4) < 3).astype(jnp.int32), jax.random.fold_in(part_splits[4], 1), 0, 1)
    w_query = noise(key_of[5], (D, D), D ** -0.5, 0.21875)
    w_key = noise(key_of[6], (D, D), D ** -0.5, 0.21875)
    w_value = noise(key_of[7], (D, D), D ** -0.5, 0.21875)
    w_gate = noise(key_of[8], (D, D), D ** -0.5, 0.21875)
    w_out = noise(key_of[9], (D, D), D ** -0.5, 0.21875)
    w_pair = noise(key_of[10], (PAIR_C, HEADS), 0.2, 1.1953125)
    rel_table = noise(key_of[11], (RELBINS, HEADS), 1.0, 6.0, (), jnp.float32)
    return {"single": single, "pair": pair, "chain": chain, "residue": residue, "valid": valid, "w_query": w_query, "w_key": w_key, "w_value": w_value, "w_gate": w_gate, "w_out": w_out, "w_pair": w_pair, "rel_table": rel_table}


NORM_EPS = 1e-05
MASK_PENALTY = 10000.0

def layer_normed(values_in):
    mean_val = lax.optimization_barrier(jnp.mean(values_in, axis=-1, keepdims=True))
    centred = values_in - mean_val
    spread = lax.optimization_barrier(jnp.mean(centred * centred, axis=-1, keepdims=True))
    return centred * lax.rsqrt(spread + NORM_EPS)

def reference(single, pair, chain, residue, valid, w_query, w_key, w_value, w_gate, w_out, w_pair, rel_table):
    token_count, sample_count, width = single.shape
    head_count = w_pair.shape[1]
    head_size = width // head_count
    channels = pair.shape[2]
    rel_bins = rel_table.shape[0]
    rel_reach = (rel_bins - 2) // 2
    normed = layer_normed(single.astype(jnp.float32)).astype(jnp.bfloat16)
    flat_rows = normed.reshape(token_count * sample_count, width)

    def project(weight):
        return jnp.dot(flat_rows, weight, preferred_element_type=jnp.float32)
    query_proj = lax.optimization_barrier(project(w_query).astype(jnp.bfloat16)).reshape(token_count, sample_count, head_count, head_size)
    key_proj = lax.optimization_barrier(project(w_key).astype(jnp.bfloat16)).reshape(token_count, sample_count, head_count, head_size)
    value_proj = lax.optimization_barrier(project(w_value).astype(jnp.bfloat16)).reshape(token_count, sample_count, head_count, head_size)
    gate_proj = jax.nn.sigmoid(project(w_gate)).reshape(token_count, sample_count, head_count, head_size)
    key_float = key_proj.astype(jnp.float32)
    value_float = value_proj.astype(jnp.float32)
    block_rows = math.gcd(token_count, 64)
    scale_factor = 1.0 / math.sqrt(head_size)
    bucket_ids = jnp.arange(rel_bins, dtype=jnp.int32)
    mask_bias = (valid.astype(jnp.float32) - 1.0) * MASK_PENALTY

    def one_block(block_index):
        start_row = (block_index * block_rows).astype(jnp.int32)
        pair_rows = lax.dynamic_slice_in_dim(pair, start_row, block_rows, 0)
        pair_bias = jnp.dot(pair_rows.reshape(block_rows * token_count, channels), w_pair, preferred_element_type=jnp.float32).reshape(block_rows, token_count, head_count)
        chain_rows = lax.dynamic_slice_in_dim(chain, start_row, block_rows, 0)
        residue_rows = lax.dynamic_slice_in_dim(residue, start_row, block_rows, 0)
        same_chain = chain_rows[:, None] == chain[None, :]
        offset = jnp.clip(residue_rows[:, None] - residue[None, :], -rel_reach, rel_reach) + rel_reach
        bucket = jnp.where(same_chain, offset, rel_bins - 1)
        one_hot = (bucket[:, :, None] == bucket_ids).astype(jnp.float32)
        rel_bias = jnp.einsum('qkb,bh->qkh', one_hot, rel_table, precision=lax.Precision.HIGHEST)
        total_bias = jnp.transpose(pair_bias + rel_bias + mask_bias[None, :, None], (2, 0, 1))
        query_rows = lax.dynamic_slice_in_dim(query_proj, start_row, block_rows, 0).astype(jnp.float32)
        scores = jnp.einsum('qshd,kshd->shqk', query_rows, key_float) * scale_factor + total_bias[None]
        top_score = lax.optimization_barrier(jnp.max(scores, axis=-1, keepdims=True))
        probs = jnp.exp(scores - top_score)
        mass = lax.optimization_barrier(jnp.sum(probs, axis=-1))
        probs_low = lax.optimization_barrier(probs.astype(jnp.bfloat16)).astype(jnp.float32)
        weighted = jnp.einsum('shqk,kshd->shqd', probs_low, value_float)
        attended = jnp.transpose(weighted / mass[..., None], (2, 0, 1, 3))
        gate_rows = lax.dynamic_slice_in_dim(gate_proj, start_row, block_rows, 0)
        gated = (gate_rows * attended).reshape(block_rows * sample_count, width).astype(jnp.bfloat16)
        out_rows = jnp.dot(gated, w_out, preferred_element_type=jnp.float32).reshape(block_rows, sample_count, width)
        single_rows = lax.dynamic_slice_in_dim(single, start_row, block_rows, 0)
        return (single_rows.astype(jnp.float32) + out_rows).astype(jnp.bfloat16)
    blocks = lax.map(one_block, jnp.arange(token_count // block_rows, dtype=jnp.int32))
    return blocks.reshape(token_count, sample_count, width)
```

```python
import functools
import math

import jax
import jax.numpy as jnp
from jax import lax
from jax.experimental import pallas as pl
from jax.experimental.pallas import tpu as pltpu
from jax.sharding import PartitionSpec as P

NORM_EPS = 1e-05
MASK_PENALTY = 10000.0
F32 = jnp.float32
BF16 = jnp.bfloat16
NT = (((1,), (1,)), ((), ()))


def normed_rows(x):
    x = x.astype(F32)
    mean = jnp.mean(x, axis=-1, keepdims=True)
    centred = x - mean
    spread = jnp.mean(centred * centred, axis=-1, keepdims=True)
    return (centred * lax.rsqrt(spread + NORM_EPS)).astype(BF16)


def kernel(
    n, ny, x_ref, meta_ref, chain_ref, residue_ref, pair_ref, wq_ref, wk_ref, wv_ref, wg_ref, wo_ref,
    wp_ref, rel_ref, out_ref,
    buf, meta_buf, mask_buf, bias_buf, q_buf, gate_buf, gated_buf,
    meta_send, meta_recv, recv, send_z, send_y, send_c,
):
    units, per, rows, width = x_ref.shape
    heads = wp_ref.shape[0]
    head_size = width // heads
    keys = n * rows
    rel_bins = rel_ref.shape[1]
    reach = (rel_bins - 2) // 2
    scale = 1.0 / math.sqrt(head_size)
    nz = n // (2 * ny)
    phases = units // 2
    me = lax.axis_index("tok")
    c = me % 2
    y = (me // 2) % ny
    z = me // (2 * ny)
    partner = me + 1 - 2 * c
    across = (z * ny + (y + 1) % ny) * 2 + c

    def place(zz, yy, cc):
        return (zz * ny + yy) * 2 + cc

    def copy(src, dst, ssem, rsem, to):
        return pltpu.make_async_remote_copy(
            src_ref=src, dst_ref=dst, send_sem=ssem, recv_sem=rsem,
            device_id={"tok": to}, device_id_type=pl.DeviceIdType.MESH,
        )

    barrier = pltpu.get_barrier_semaphore()

    @pl.loop(1, n)
    def _(k):
        pl.semaphore_signal(
            barrier, inc=1, device_id={"tok": (me + k) % n}, device_id_type=pl.DeviceIdType.MESH
        )

    pl.semaphore_wait(barrier, n - 1)

    def first_copy(p, k):
        g = k % 2
        zz = (z + k // 2) % nz
        to = place(zz, y, (c + g) % 2)
        u = 2 * p + (c + g) % 2
        return copy(x_ref.at[u], buf.at[u, me], send_z.at[p, k], recv.at[u, me], to)

    def own_across(p):
        u = 2 * p + c
        return copy(x_ref.at[u], buf.at[u, me], send_y.at[p, 0], recv.at[u, me], across)

    def own_partner(p):
        u = 2 * p + c
        return copy(x_ref.at[u], buf.at[u, me], send_c.at[p, 0], recv.at[u, me], partner)

    def source(k):
        return place((z + k // 2) % nz, y, (c + k) % 2)

    def source_across(k):
        return place((z + k // 2) % nz, (y + 1) % ny, (c + k) % 2)

    def forward_across(p, k):
        u = 2 * p + c
        j = source(k)
        return copy(buf.at[u, j], buf.at[u, j], send_y.at[p, k], recv.at[u, j], across)

    def forward_partner(p, k):
        u = 2 * p + c
        j = source(k)
        return copy(buf.at[u, j], buf.at[u, j], send_c.at[p, k], recv.at[u, j], partner)

    def forward_partner_across(p, k):
        u = 2 * p + c
        j = source_across(k)
        return copy(
            buf.at[u, j], buf.at[u, j], send_c.at[p, 2 * nz + k], recv.at[u, j], partner
        )

    def wait_unit(u, j):
        copy(buf.at[u, j], buf.at[u, j], send_c.at[0, 0], recv.at[u, j], partner).wait_recv()

    def start_phase(p):
        own_across(p).start()

        @pl.loop(1, 2 * nz)
        def _(k):
            first_copy(p, k).start()

        own_partner(p).start()

    def pass_on(p):
        @pl.loop(1, 2 * nz)
        def _(k):
            wait_unit(2 * p + c, source(k))
            forward_across(p, k).start()

            @pl.when(k != 1)
            def _():
                forward_partner(p, k).start()

    def pass_back(p):
        @pl.loop(0, 2 * nz)
        def _(k):
            wait_unit(2 * p + c, source_across(k))
            forward_partner_across(p, k).start()

    def finish_phase(p):
        @pl.loop(1, n)
        def _(k):
            wait_unit(2 * p + 1 - c, (me + k) % n)

    def meta_copy(k):
        to = (me + k) % n
        return copy(meta_ref, meta_buf.at[me], meta_send.at[k], meta_recv.at[me], to)

    @pl.loop(1, n)
    def _(k):
        meta_copy(k).start()

    start_phase(0)

    for u in range(units):
        buf[u, me] = x_ref[u]
    meta_buf[me] = meta_ref[...]
    own = normed_rows(x_ref[...].reshape(units * per * rows, width))
    q_buf[...] = jnp.dot(own, wq_ref[...], preferred_element_type=F32).astype(BF16).reshape(
        units * per, rows, width
    )
    gate_buf[...] = jax.nn.sigmoid(
        jnp.dot(own, wg_ref[...], preferred_element_type=F32)
    ).reshape(units * per, rows, width)
    lane_head = lax.broadcasted_iota(jnp.int32, (heads, rows, width), 2) // head_size
    row_head = lax.broadcasted_iota(jnp.int32, (heads, rows, width), 0)
    mask_buf[...] = (lane_head == row_head).astype(F32).astype(BF16)

    pass_on(0)
    for p in range(1, phases):
        start_phase(p)

    @pl.loop(1, n)
    def _(k):
        j = (me + k) % n
        copy(meta_ref, meta_buf.at[j], meta_send.at[k], meta_recv.at[j], j).wait_recv()

    lanes = meta_ref.shape[1]
    spread_to = (
        lax.broadcasted_iota(jnp.int32, (lanes, keys), 0)
        == lax.broadcasted_iota(jnp.int32, (lanes, keys), 1) % rows
    ).astype(F32)
    tiled = jnp.dot(
        meta_buf[...].reshape(n * 8, lanes), spread_to,
        precision=lax.Precision.HIGHEST, preferred_element_type=F32,
    ).reshape(n, 8, keys)
    owner = lax.broadcasted_iota(jnp.int32, (n, 8, keys), 2) // rows
    block = lax.broadcasted_iota(jnp.int32, (n, 8, keys), 0)
    meta_all = jnp.sum(jnp.where(owner == block, tiled, 0.0), axis=0)
    chain_keys = meta_all[0:1].astype(jnp.int32)
    residue_keys = meta_all[1:2].astype(jnp.int32)
    penalty = (meta_all[2:3] - 1.0) * MASK_PENALTY
    table = rel_ref[...]
    high = table.astype(BF16)
    left = table - high.astype(F32)
    middle = left.astype(BF16)
    low = (left - middle.astype(F32)).astype(BF16)
    table3 = jnp.concatenate([high, middle, low], axis=0)
    bins = lax.broadcasted_iota(jnp.int32, (rel_bins, keys), 0)
    for q in range(rows):
        offset = jnp.clip(residue_ref[q] - residue_keys, -reach, reach) + reach
        bucket = jnp.where(chain_ref[q] == chain_keys, offset, rel_bins - 1)
        hot = (bucket == bins).astype(F32).astype(BF16)
        rel3 = jnp.dot(table3, hot, preferred_element_type=F32)
        rel = rel3[:heads] + rel3[heads : 2 * heads] + rel3[2 * heads :]
        pb = lax.dot_general(wp_ref[...], pair_ref[q], NT, preferred_element_type=F32)
        bias_buf[:, q, :] = pb + rel + penalty

    def attend(u, i):
        s = u * per + i
        x = normed_rows(buf[u, :, i].reshape(keys, width))
        key = jnp.dot(x, wk_ref[...], preferred_element_type=F32).astype(BF16)
        value = jnp.dot(x, wv_ref[...], preferred_element_type=F32).astype(BF16)
        mask = mask_buf[...]
        query = (mask * q_buf[s][None]).reshape(heads * rows, width)
        scores = lax.dot_general(query, key, NT, preferred_element_type=F32) * scale
        scores = scores + bias_buf[...].reshape(heads * rows, keys)
        probs = jnp.exp(scores - jnp.max(scores, axis=-1, keepdims=True))
        mass = jnp.sum(probs, axis=-1, keepdims=True)
        got = jnp.dot(probs.astype(BF16), value, preferred_element_type=F32) * (1.0 / mass)
        got = jnp.sum(got.reshape(heads, rows, width) * mask.astype(F32), axis=0)
        gated_buf[s] = (gate_buf[s] * got).astype(BF16)

    pass_back(0)
    for p in range(phases):
        if p + 1 < phases:
            pass_on(p + 1)
        finish_phase(p)
        if p + 1 < phases:
            attend(2 * p, 0)
            pass_back(p + 1)
            for i in range(1, per):
                attend(2 * p, i)
        else:
            for i in range(per):
                attend(2 * p, i)
        for i in range(per):
            attend(2 * p + 1, i)

    gated = gated_buf[...].reshape(units * per * rows, width)
    out = jnp.dot(gated, wo_ref[...], preferred_element_type=F32)
    out = out.reshape(units, per, rows, width) + x_ref[...].astype(F32)
    out_ref[...] = out.astype(BF16)

    @pl.loop(1, n)
    def _(k):
        meta_copy(k).wait_send()

    for p in range(phases):
        own_across(p).wait_send()
        own_partner(p).wait_send()

        @pl.loop(1, 2 * nz)
        def _(k):
            first_copy(p, k).wait_send()
            forward_across(p, k).wait_send()

            @pl.when(k != 1)
            def _():
                forward_partner(p, k).wait_send()

        @pl.loop(0, 2 * nz)
        def _(k):
            forward_partner_across(p, k).wait_send()


def shards(
    single, pair, chain, residue, valid, w_query, w_key, w_value, w_gate, w_out, w_pair, rel_table
):
    rows, samples, width = single.shape
    n = lax.axis_size("tok")
    ny = 2
    nz = n // (2 * ny)
    units = 4
    per = samples // units
    heads = w_pair.shape[1]
    keys = pair.shape[1]
    x = jnp.transpose(single, (1, 0, 2)).reshape(units, per, rows, width)
    lanes = -(-rows // 128) * 128
    meta = jnp.pad(
        jnp.stack([chain, residue, valid]).astype(F32), ((0, 5), (0, lanes - rows))
    )
    vmem = pl.BlockSpec(memory_space=pltpu.VMEM)
    smem = pl.BlockSpec(memory_space=pltpu.SMEM)
    phases = units // 2
    out = pl.pallas_call(
        functools.partial(kernel, n, ny),
        out_shape=jax.ShapeDtypeStruct(x.shape, BF16),
        in_specs=[vmem, vmem, smem, smem] + [vmem] * 8,
        out_specs=vmem,
        scratch_shapes=[
            pltpu.VMEM((units, n, per, rows, width), BF16),
            pltpu.VMEM((n, 8, lanes), F32),
            pltpu.VMEM((heads, rows, width), BF16),
            pltpu.VMEM((heads, rows, keys), F32),
            pltpu.VMEM((samples, rows, width), BF16),
            pltpu.VMEM((samples, rows, width), F32),
            pltpu.VMEM((samples, rows, width), BF16),
            pltpu.SemaphoreType.DMA((n,)),
            pltpu.SemaphoreType.DMA((n,)),
            pltpu.SemaphoreType.DMA((units, n)),
            pltpu.SemaphoreType.DMA((phases, 2 * nz)),
            pltpu.SemaphoreType.DMA((phases, 2 * nz)),
            pltpu.SemaphoreType.DMA((phases, n)),
        ],
        compiler_params=pltpu.CompilerParams(
            collective_id=0, has_side_effects=True, vmem_limit_bytes=56 * 1024 * 1024
        ),
        cost_estimate=pl.CostEstimate(
            flops=7 * 10**9, bytes_accessed=10**7, transcendentals=10**6
        ),
    )(x, meta, chain, residue, pair, w_query, w_key, w_value, w_gate, w_out, w_pair.T, rel_table.T)
    return jnp.transpose(out.reshape(samples, rows, width), (1, 0, 2))


def solution(mesh):
    split = P(("groups", "tok"))
    rows = P(("groups", "tok"), None, None)
    return jax.shard_map(
        shards,
        mesh=mesh,
        in_specs=(rows, rows, split, split, split) + (P(),) * 7,
        out_specs=rows,
        check_vma=False,
    )
```

```python
import functools
import math

import jax
import jax.numpy as jnp
from jax import lax
from jax.experimental import pallas as pl
from jax.experimental.pallas import tpu as pltpu
from jax.sharding import PartitionSpec as P

NORM_EPS = 1e-05
MASK_PENALTY = 10000.0
F32 = jnp.float32
BF16 = jnp.bfloat16
NT = (((1,), (1,)), ((), ()))


def normed_rows(x):
    x = x.astype(F32)
    mean = jnp.mean(x, axis=-1, keepdims=True)
    centred = x - mean
    spread = jnp.mean(centred * centred, axis=-1, keepdims=True)
    return (centred * lax.rsqrt(spread + NORM_EPS)).astype(BF16)


def kernel(
    n, ny, single_ref, chain_row, residue_row, valid_row, chain_ref, residue_ref, wp_ref, rel_ref,
    pair_hbm, wq_hbm, wk_hbm, wv_hbm, wg_hbm, wo_hbm, out_ref,
    buf, x_ref, meta_ref, meta_buf, mask_buf, bias_buf, q_buf, gate_buf, gated_buf, wide_buf,
    pair_ref, wq_ref, wk_ref, wv_ref, wg_ref, wo_ref,
    load, meta_send, meta_recv, recv, send_x, send_up, send_down, send_y, send_c,
):
    units, per, rows, width = x_ref.shape
    heads = wp_ref.shape[0]
    head_size = width // heads
    keys = n * rows
    rel_bins = rel_ref.shape[1]
    reach = (rel_bins - 2) // 2
    scale = 1.0 / math.sqrt(head_size)
    nz = n // (2 * ny)
    phases = units // 2
    me = lax.axis_index("tok")
    c = me % 2
    y = (me // 2) % ny
    z = me // (2 * ny)

    def place(zz, yy, cc):
        return (zz * ny + yy) * 2 + cc

    partner = place(z, y, 1 - c)
    across = place(z, (y + 1) % ny, c)
    above = place((z + 1) % nz, y, c)
    below = place((z + nz - 1) % nz, y, c)
    loads = [
        pltpu.make_async_copy(src, dst, load.at[i])
        for i, (src, dst) in enumerate(
            [
                (wq_hbm, wq_ref), (wg_hbm, wg_ref), (pair_hbm, pair_ref),
                (wk_hbm, wk_ref), (wv_hbm, wv_ref), (wo_hbm, wo_ref),
            ]
        )
    ]
    barrier = pltpu.get_barrier_semaphore()
    for to in (above, below, across, partner):
        pl.semaphore_signal(
            barrier, inc=1, device_id={"tok": to}, device_id_type=pl.DeviceIdType.MESH
        )
    wide_buf[...] = single_ref[...].astype(F32)
    for s in range(units * per):
        x_ref[s // per, s % per] = wide_buf[:, s, :].astype(BF16)
    meta_ref[...] = jnp.zeros_like(meta_ref)
    meta_ref[0:1, 0:rows] = chain_row[...].astype(F32)
    meta_ref[1:2, 0:rows] = residue_row[...].astype(F32)
    meta_ref[2:3, 0:rows] = valid_row[...].astype(F32)
    for u in range(units):
        buf[u, me] = x_ref[u]
    meta_buf[me] = meta_ref[...]
    pl.semaphore_wait(barrier, 4)

    def copy(src, dst, ssem, rsem, to):
        return pltpu.make_async_remote_copy(
            src_ref=src, dst_ref=dst, send_sem=ssem, recv_sem=rsem,
            device_id={"tok": to}, device_id_type=pl.DeviceIdType.MESH,
        )

    def block(u, j, ssem, to):
        return copy(buf.at[u, j], buf.at[u, j], ssem, recv.at[u, j], to)

    def meta_block(j, way, to):
        return copy(meta_buf.at[j], meta_buf.at[j], meta_send.at[way, j], meta_recv.at[j], to)

    def when(cond, fn):
        pl.when(cond)(fn)

    def routes(p, dz, go, cc, act, first):
        zz = z + dz
        j = place(zz, y, cc)
        u = 2 * p + c
        slot = zz * 2 + cc

        def along():
            if go >= 0:
                when(z < nz - 1, lambda: act(block(u, j, send_up.at[p, slot], above)))
            if go <= 0:
                when(z > 0, lambda: act(block(u, j, send_down.at[p, slot], below)))

        along()
        act(block(u, j, send_y.at[p, slot], across))
        if not first:
            act(block(u, j, send_c.at[p, j], partner))

    def meta_routes(dz, go, act):
        j = place(z + dz, y, c)
        if go >= 0:
            when(z < nz - 1, lambda: act(meta_block(j, 0, above)))
        if go <= 0:
            when(z > 0, lambda: act(meta_block(j, 1, below)))
        act(meta_block(j, 2, across))
        act(meta_block(j, 3, partner))

    def start(op):
        op.start()

    def end(op):
        op.wait_send()

    def wait_unit(u, j):
        block(u, j, send_c.at[0, 0], partner).wait_recv()

    def wait_meta(j):
        meta_block(j, 0, partner).wait_recv()

    def own_out(p, act):
        act(block(2 * p + 1 - c, me, send_x.at[p], partner))
        routes(p, 0, 0, c, act, False)

    def partner_out(p, act, wait):
        if wait:
            wait_unit(2 * p + c, partner)
        routes(p, 0, 0, 1 - c, act, True)

    def hop(p, h, act, wait):
        def from_below():
            if p == 0:
                if wait:
                    wait_meta(place(z - h, y, c))
                meta_routes(-h, 1, act)
            for cc in (c, 1 - c):
                if wait:
                    wait_unit(2 * p + c, place(z - h, y, cc))
                routes(p, -h, 1, cc, act, False)

        def from_above():
            if p == 0:
                if wait:
                    wait_meta(place(z + h, y, c))
                meta_routes(h, -1, act)
            for cc in (c, 1 - c):
                if wait:
                    wait_unit(2 * p + c, place(z + h, y, cc))
                routes(p, h, -1, cc, act, False)

        when(z - h >= 0, from_below)
        when(z + h < nz, from_above)

    def back(p, dz, act, wait):
        def go():
            if p == 0:
                j = place(z + dz, (y + 1) % ny, c)
                if wait:
                    wait_meta(j)
                act(meta_block(j, 3, partner))
            for cc in (c, 1 - c):
                j = place(z + dz, (y + 1) % ny, cc)
                if wait:
                    wait_unit(2 * p + c, j)
                act(block(2 * p + c, j, send_c.at[p, j], partner))

        when((z + dz >= 0) & (z + dz < nz), go)

    def backs(p, h, act, wait):
        back(p, h, act, wait)
        back(p, -h, act, wait)

    def hops(p, low, high, act=start, wait=True):
        if high - low <= 4:
            for h in range(low, high):
                hop(p, h, act, wait)
        else:
            pl.loop(low, high)(lambda h: hop(p, h, act, wait))

    def all_backs(p, low, high, act=start, wait=True):
        if high - low <= 4:
            for h in range(low, high):
                backs(p, h, act, wait)
        else:
            pl.loop(low, high)(lambda h: backs(p, h, act, wait))

    def finish_phase(p):
        @pl.loop(1, n)
        def _(k):
            j = (me + k) % n

            @pl.when(j != partner)
            def _():
                wait_unit(2 * p + 1 - c, j)

        wait_unit(2 * p + 1 - c, partner)

    meta_routes(0, 0, start)
    for p in range(phases):
        own_out(p, start)
    for op in loads:
        op.start()
    for p in range(phases):
        partner_out(p, start, True)
    own = normed_rows(x_ref[...].reshape(units * per * rows, width))
    lane_head = lax.broadcasted_iota(jnp.int32, (heads, rows, width), 2) // head_size
    row_head = lax.broadcasted_iota(jnp.int32, (heads, rows, width), 0)
    mask_buf[...] = (lane_head == row_head).astype(F32).astype(BF16)
    loads[0].wait()
    q_buf[...] = jnp.dot(own, wq_ref[...], preferred_element_type=F32).astype(BF16).reshape(
        units * per, rows, width
    )
    hops(0, 1, 2)
    hops(1, 1, 2)
    back(0, 0, start, True)
    loads[1].wait()
    gate_buf[...] = jax.nn.sigmoid(
        jnp.dot(own, wg_ref[...], preferred_element_type=F32)
    ).reshape(units * per, rows, width)
    hops(0, 2, nz)
    back(1, 0, start, True)
    hops(1, 2, min(3, nz))
    all_backs(0, 1, nz)

    @pl.loop(0, nz * ny)
    def _(k):
        wait_meta(k * 2 + 1 - c)

    for op in loads[2:]:
        op.wait()
    lanes = meta_ref.shape[1]
    spread_to = (
        lax.broadcasted_iota(jnp.int32, (lanes, keys), 0)
        == lax.broadcasted_iota(jnp.int32, (lanes, keys), 1) % rows
    ).astype(F32)
    tiled = jnp.dot(
        meta_buf[...].reshape(n * 8, lanes), spread_to,
        precision=lax.Precision.HIGHEST, preferred_element_type=F32,
    ).reshape(n, 8, keys)
    owner = lax.broadcasted_iota(jnp.int32, (n, 8, keys), 2) // rows
    holder = lax.broadcasted_iota(jnp.int32, (n, 8, keys), 0)
    meta_all = jnp.sum(jnp.where(owner == holder, tiled, 0.0), axis=0)
    chain_keys = meta_all[0:1].astype(jnp.int32)
    residue_keys = meta_all[1:2].astype(jnp.int32)
    penalty = (meta_all[2:3] - 1.0) * MASK_PENALTY
    table = rel_ref[...]
    high = table.astype(BF16)
    left = table - high.astype(F32)
    middle = left.astype(BF16)
    low = (left - middle.astype(F32)).astype(BF16)
    table3 = jnp.concatenate([high, middle, low], axis=0)
    bins = lax.broadcasted_iota(jnp.int32, (rel_bins, keys), 0)
    for q in range(rows):
        offset = jnp.clip(residue_ref[q] - residue_keys, -reach, reach) + reach
        bucket = jnp.where(chain_ref[q] == chain_keys, offset, rel_bins - 1)
        hot = (bucket == bins).astype(F32).astype(BF16)
        rel3 = jnp.dot(table3, hot, preferred_element_type=F32)
        rel = rel3[:heads] + rel3[heads : 2 * heads] + rel3[2 * heads :]
        pb = lax.dot_general(wp_ref[...], pair_ref[q], NT, preferred_element_type=F32)
        bias_buf[:, q, :] = pb + rel + penalty

    def attend(u, i):
        s = u * per + i
        x = normed_rows(buf[u, :, i].reshape(keys, width))
        key = jnp.dot(x, wk_ref[...], preferred_element_type=F32).astype(BF16)
        value = jnp.dot(x, wv_ref[...], preferred_element_type=F32).astype(BF16)
        mask = mask_buf[...]
        query = (mask * q_buf[s][None]).reshape(heads * rows, width)
        scores = lax.dot_general(query, key, NT, preferred_element_type=F32) * scale
        scores = scores + bias_buf[...].reshape(heads * rows, keys)
        probs = jnp.exp(scores - jnp.max(scores, axis=-1, keepdims=True))
        mass = jnp.sum(probs, axis=-1, keepdims=True)
        got = jnp.dot(probs.astype(BF16), value, preferred_element_type=F32) * (1.0 / mass)
        got = jnp.sum(got.reshape(heads, rows, width) * mask.astype(F32), axis=0)
        gated_buf[s] = (gate_buf[s] * got).astype(BF16)

    hops(1, min(3, nz), nz)
    finish_phase(0)
    attend(0, 0)
    all_backs(1, 1, nz)
    for i in range(1, per):
        attend(0, i)
    for i in range(per):
        attend(1, i)
    for p in range(1, phases):
        finish_phase(p)
        for i in range(per):
            attend(2 * p, i)
        for i in range(per):
            attend(2 * p + 1, i)

    gated = gated_buf[...].reshape(units * per * rows, width)
    out = jnp.dot(gated, wo_ref[...], preferred_element_type=F32)
    out = out.reshape(units * per, rows, width)
    for s in range(units * per):
        wide_buf[:, s, :] = wide_buf[:, s, :] + out[s]
    out_ref[...] = wide_buf[...].astype(BF16)

    meta_routes(0, 0, end)
    for p in range(phases):
        own_out(p, end)
        partner_out(p, end, False)
        hops(p, 1, nz, end, False)
        back(p, 0, end, False)
        all_backs(p, 1, nz, end, False)


def shards(
    single, pair, chain, residue, valid, w_query, w_key, w_value, w_gate, w_out, w_pair, rel_table
):
    rows, samples, width = single.shape
    n = lax.axis_size("tok")
    ny = 2
    nz = n // (2 * ny)
    units = 4
    per = samples // units
    heads = w_pair.shape[1]
    keys = pair.shape[1]
    lanes = -(-rows // 128) * 128
    vmem = pl.BlockSpec(memory_space=pltpu.VMEM)
    smem = pl.BlockSpec(memory_space=pltpu.SMEM)
    hbm = pl.BlockSpec(memory_space=pl.ANY)
    phases = units // 2
    weight = pltpu.VMEM(w_query.shape, BF16)
    dma = pltpu.SemaphoreType.DMA
    return pl.pallas_call(
        functools.partial(kernel, n, ny),
        out_shape=jax.ShapeDtypeStruct(single.shape, BF16),
        in_specs=[vmem] * 4 + [smem] * 2 + [vmem] * 2 + [hbm] * 6,
        out_specs=vmem,
        scratch_shapes=[
            pltpu.VMEM((units, n, per, rows, width), BF16),
            pltpu.VMEM((units, per, rows, width), BF16),
            pltpu.VMEM((8, lanes), F32),
            pltpu.VMEM((n, 8, lanes), F32),
            pltpu.VMEM((heads, rows, width), BF16),
            pltpu.VMEM((heads, rows, keys), F32),
            pltpu.VMEM((samples, rows, width), BF16),
            pltpu.VMEM((samples, rows, width), F32),
            pltpu.VMEM((samples, rows, width), BF16),
            pltpu.VMEM((rows, samples, width), F32),
            pltpu.VMEM(pair.shape, BF16),
            weight, weight, weight, weight, weight,
            dma((6,)),
            dma((4, n)),
            dma((n,)),
            dma((units, n)),
            dma((phases,)),
            dma((phases, 2 * nz)),
            dma((phases, 2 * nz)),
            dma((phases, 2 * nz)),
            dma((phases, n)),
        ],
        compiler_params=pltpu.CompilerParams(
            collective_id=0, has_side_effects=True, vmem_limit_bytes=56 * 1024 * 1024
        ),
        cost_estimate=pl.CostEstimate(
            flops=7 * 10**9, bytes_accessed=10**7, transcendentals=10**6
        ),
    )(
        single, chain.reshape(1, rows), residue.reshape(1, rows), valid.reshape(1, rows),
        chain, residue, w_pair.T, rel_table.T, pair, w_query, w_key, w_value, w_gate, w_out,
    )


def solution(mesh):
    split = P(("groups", "tok"))
    rows = P(("groups", "tok"), None, None)
    return jax.shard_map(
        shards,
        mesh=mesh,
        in_specs=(rows, rows, split, split, split) + (P(),) * 7,
        out_specs=rows,
        check_vma=False,
    )
```

```python
import functools
import math

import jax
import jax.numpy as jnp
from jax import lax
from jax.experimental import pallas as pl
from jax.experimental.pallas import tpu as pltpu
from jax.sharding import PartitionSpec as P

NORM_EPS = 1e-05
MASK_PENALTY = 10000.0
F32 = jnp.float32
BF16 = jnp.bfloat16
NT = (((1,), (1,)), ((), ()))


def normed_rows(x):
    x = x.astype(F32)
    mean = jnp.mean(x, axis=-1, keepdims=True)
    centred = x - mean
    spread = jnp.mean(centred * centred, axis=-1, keepdims=True)
    return (centred * lax.rsqrt(spread + NORM_EPS)).astype(BF16)


def kernel(
    n, ny, single_ref, chain_row, residue_row, valid_row, chain_ref, residue_ref, wp_ref, rel_ref,
    pair_hbm, wq_hbm, wk_hbm, wv_hbm, wg_hbm, wo_hbm, out_ref,
    buf, x_ref, meta_ref, meta_buf, mask_buf, bias_buf, q_buf, gate_buf, gated_buf, wide_buf,
    pair_ref, wq_ref, wk_ref, wv_ref, wg_ref, wo_ref,
    load, meta_send, meta_recv, recv, send_x, send_up, send_down, send_y, send_c,
):
    units, per, rows, width = x_ref.shape
    heads = wp_ref.shape[0]
    head_size = width // heads
    keys = n * rows
    rel_bins = rel_ref.shape[1]
    reach = (rel_bins - 2) // 2
    scale = 1.0 / math.sqrt(head_size)
    nz = n // (2 * ny)
    phases = units // 2
    me = lax.axis_index("tok")
    c = me % 2
    y = (me // 2) % ny
    z = me // (2 * ny)

    def place(zz, yy, cc):
        return (zz * ny + yy) * 2 + cc

    partner = place(z, y, 1 - c)
    across = place(z, (y + 1) % ny, c)
    above = place((z + 1) % nz, y, c)
    below = place((z + nz - 1) % nz, y, c)
    loads = [
        pltpu.make_async_copy(src, dst, load.at[i])
        for i, (src, dst) in enumerate(
            [
                (wq_hbm, wq_ref), (wg_hbm, wg_ref), (pair_hbm, pair_ref),
                (wk_hbm, wk_ref), (wv_hbm, wv_ref), (wo_hbm, wo_ref),
            ]
        )
    ]
    barrier = pltpu.get_barrier_semaphore()
    for to in (above, below, across, partner):
        pl.semaphore_signal(
            barrier, inc=1, device_id={"tok": to}, device_id_type=pl.DeviceIdType.MESH
        )
    wide_buf[...] = single_ref[...].astype(F32)
    for s in range(units * per):
        x_ref[s // per, s % per] = wide_buf[:, s, :].astype(BF16)
    meta_ref[...] = jnp.zeros_like(meta_ref)
    meta_ref[0:1, 0:rows] = chain_row[...].astype(F32)
    meta_ref[1:2, 0:rows] = residue_row[...].astype(F32)
    meta_ref[2:3, 0:rows] = valid_row[...].astype(F32)
    for u in range(units):
        buf[u, me] = x_ref[u]
    meta_buf[me] = meta_ref[...]
    pl.semaphore_wait(barrier, 4)

    def copy(src, dst, ssem, rsem, to):
        return pltpu.make_async_remote_copy(
            src_ref=src, dst_ref=dst, send_sem=ssem, recv_sem=rsem,
            device_id={"tok": to}, device_id_type=pl.DeviceIdType.MESH,
        )

    def block(u, j, ssem, to):
        return copy(buf.at[u, j], buf.at[u, j], ssem, recv.at[u, j], to)

    def meta_block(j, way, to):
        return copy(meta_buf.at[j], meta_buf.at[j], meta_send.at[way, j], meta_recv.at[j], to)

    def when(cond, fn):
        pl.when(cond)(fn)

    def routes(p, dz, go, cc, act, first):
        zz = z + dz
        j = place(zz, y, cc)
        u = 2 * p + c
        slot = zz * 2 + cc

        def along():
            if go >= 0:
                when(z < nz - 1, lambda: act(block(u, j, send_up.at[p, slot], above)))
            if go <= 0:
                when(z > 0, lambda: act(block(u, j, send_down.at[p, slot], below)))

        along()
        act(block(u, j, send_y.at[p, slot], across))
        if not first:
            act(block(u, j, send_c.at[p, j], partner))

    def meta_routes(dz, go, act):
        j = place(z + dz, y, c)
        if go >= 0:
            when(z < nz - 1, lambda: act(meta_block(j, 0, above)))
        if go <= 0:
            when(z > 0, lambda: act(meta_block(j, 1, below)))
        act(meta_block(j, 2, across))
        act(meta_block(j, 3, partner))

    def start(op):
        op.start()

    def end(op):
        op.wait_send()

    def wait_unit(u, j):
        block(u, j, send_c.at[0, 0], partner).wait_recv()

    def wait_meta(j):
        meta_block(j, 0, partner).wait_recv()

    def own_out(p, act):
        act(block(2 * p + 1 - c, me, send_x.at[p], partner))
        routes(p, 0, 0, c, act, False)

    def partner_out(p, act, wait):
        if wait:
            wait_unit(2 * p + c, partner)
        routes(p, 0, 0, 1 - c, act, True)

    def hop(p, h, act, wait):
        def from_below():
            if p == 0:
                if wait:
                    wait_meta(place(z - h, y, c))
                meta_routes(-h, 1, act)
            for cc in (c, 1 - c):
                if wait:
                    wait_unit(2 * p + c, place(z - h, y, cc))
                routes(p, -h, 1, cc, act, False)

        def from_above():
            if p == 0:
                if wait:
                    wait_meta(place(z + h, y, c))
                meta_routes(h, -1, act)
            for cc in (c, 1 - c):
                if wait:
                    wait_unit(2 * p + c, place(z + h, y, cc))
                routes(p, h, -1, cc, act, False)

        when(z - h >= 0, from_below)
        when(z + h < nz, from_above)

    def back(p, dz, act, wait):
        def go():
            if p == 0:
                j = place(z + dz, (y + 1) % ny, c)
                if wait:
                    wait_meta(j)
                act(meta_block(j, 3, partner))
            for cc in (c, 1 - c):
                j = place(z + dz, (y + 1) % ny, cc)
                if wait:
                    wait_unit(2 * p + c, j)
                act(block(2 * p + c, j, send_c.at[p, j], partner))

        when((z + dz >= 0) & (z + dz < nz), go)

    def backs(p, h, act, wait):
        back(p, h, act, wait)
        back(p, -h, act, wait)

    def hops(p, low, high, act=start, wait=True):
        if high - low <= 4:
            for h in range(low, high):
                hop(p, h, act, wait)
        else:
            pl.loop(low, high)(lambda h: hop(p, h, act, wait))

    def all_backs(p, low, high, act=start, wait=True):
        if high - low <= 4:
            for h in range(low, high):
                backs(p, h, act, wait)
        else:
            pl.loop(low, high)(lambda h: backs(p, h, act, wait))

    def finish_phase(p):
        @pl.loop(1, n)
        def _(k):
            j = (me + k) % n

            @pl.when(j != partner)
            def _():
                wait_unit(2 * p + 1 - c, j)

        wait_unit(2 * p + 1 - c, partner)

    meta_routes(0, 0, start)
    for p in range(phases):
        own_out(p, start)
    for op in loads:
        op.start()
    for p in range(phases):
        partner_out(p, start, True)
    own = normed_rows(x_ref[...].reshape(units * per * rows, width))
    lane_head = lax.broadcasted_iota(jnp.int32, (heads, rows, width), 2) // head_size
    row_head = lax.broadcasted_iota(jnp.int32, (heads, rows, width), 0)
    mask_buf[...] = (lane_head == row_head).astype(F32).astype(BF16)
    loads[0].wait()
    q_buf[...] = jnp.dot(own, wq_ref[...], preferred_element_type=F32).astype(BF16).reshape(
        units * per, rows, width
    )
    hops(0, 1, 2)
    hops(1, 1, 2)
    back(0, 0, start, True)
    loads[1].wait()
    gate_buf[...] = jax.nn.sigmoid(
        jnp.dot(own, wg_ref[...], preferred_element_type=F32)
    ).reshape(units * per, rows, width)
    hops(0, 2, min(3, nz))
    hops(1, 2, min(3, nz))
    back(1, 0, start, True)
    hops(0, min(3, nz), nz)
    hops(1, min(3, nz), nz)
    all_backs(0, 1, nz)

    @pl.loop(0, nz * ny)
    def _(k):
        wait_meta(k * 2 + 1 - c)

    for op in loads[2:]:
        op.wait()
    lanes = meta_ref.shape[1]
    spread_to = (
        lax.broadcasted_iota(jnp.int32, (lanes, keys), 0)
        == lax.broadcasted_iota(jnp.int32, (lanes, keys), 1) % rows
    ).astype(F32)
    tiled = jnp.dot(
        meta_buf[...].reshape(n * 8, lanes), spread_to,
        precision=lax.Precision.HIGHEST, preferred_element_type=F32,
    ).reshape(n, 8, keys)
    owner = lax.broadcasted_iota(jnp.int32, (n, 8, keys), 2) // rows
    holder = lax.broadcasted_iota(jnp.int32, (n, 8, keys), 0)
    meta_all = jnp.sum(jnp.where(owner == holder, tiled, 0.0), axis=0)
    chain_keys = meta_all[0:1].astype(jnp.int32)
    residue_keys = meta_all[1:2].astype(jnp.int32)
    penalty = (meta_all[2:3] - 1.0) * MASK_PENALTY
    table = rel_ref[...]
    high = table.astype(BF16)
    left = table - high.astype(F32)
    middle = left.astype(BF16)
    low = (left - middle.astype(F32)).astype(BF16)
    table3 = jnp.concatenate([high, middle, low], axis=0)
    bins = lax.broadcasted_iota(jnp.int32, (rel_bins, keys), 0)
    for q in range(rows):
        offset = jnp.clip(residue_ref[q] - residue_keys, -reach, reach) + reach
        bucket = jnp.where(chain_ref[q] == chain_keys, offset, rel_bins - 1)
        hot = (bucket == bins).astype(F32).astype(BF16)
        rel3 = jnp.dot(table3, hot, preferred_element_type=F32)
        rel = rel3[:heads] + rel3[heads : 2 * heads] + rel3[2 * heads :]
        pb = lax.dot_general(wp_ref[...], pair_ref[q], NT, preferred_element_type=F32)
        bias_buf[:, q, :] = pb + rel + penalty

    def attend(u, i):
        s = u * per + i
        x = normed_rows(buf[u, :, i].reshape(keys, width))
        key = jnp.dot(x, wk_ref[...], preferred_element_type=F32).astype(BF16)
        value = jnp.dot(x, wv_ref[...], preferred_element_type=F32).astype(BF16)
        mask = mask_buf[...]
        query = (mask * q_buf[s][None]).reshape(heads * rows, width)
        scores = lax.dot_general(query, key, NT, preferred_element_type=F32) * scale
        scores = scores + bias_buf[...].reshape(heads * rows, keys)
        probs = jnp.exp(scores - jnp.max(scores, axis=-1, keepdims=True))
        mass = jnp.sum(probs, axis=-1, keepdims=True)
        got = jnp.dot(probs.astype(BF16), value, preferred_element_type=F32) * (1.0 / mass)
        got = jnp.sum(got.reshape(heads, rows, width) * mask.astype(F32), axis=0)
        gated_buf[s] = (gate_buf[s] * got).astype(BF16)

    finish_phase(0)
    attend(0, 0)
    all_backs(1, 1, nz)
    for i in range(1, per):
        attend(0, i)
    for i in range(per):
        attend(1, i)
    for p in range(1, phases):
        finish_phase(p)
        for i in range(per):
            attend(2 * p, i)
        for i in range(per):
            attend(2 * p + 1, i)

    gated = gated_buf[...].reshape(units * per * rows, width)
    out = jnp.dot(gated, wo_ref[...], preferred_element_type=F32)
    out = out.reshape(units * per, rows, width)
    for s in range(units * per):
        wide_buf[:, s, :] = wide_buf[:, s, :] + out[s]
    out_ref[...] = wide_buf[...].astype(BF16)

    meta_routes(0, 0, end)
    for p in range(phases):
        own_out(p, end)
        partner_out(p, end, False)
        hops(p, 1, nz, end, False)
        back(p, 0, end, False)
        all_backs(p, 1, nz, end, False)


def shards(
    single, pair, chain, residue, valid, w_query, w_key, w_value, w_gate, w_out, w_pair, rel_table
):
    rows, samples, width = single.shape
    n = lax.axis_size("tok")
    ny = 2
    nz = n // (2 * ny)
    units = 4
    per = samples // units
    heads = w_pair.shape[1]
    keys = pair.shape[1]
    lanes = -(-rows // 128) * 128
    vmem = pl.BlockSpec(memory_space=pltpu.VMEM)
    smem = pl.BlockSpec(memory_space=pltpu.SMEM)
    hbm = pl.BlockSpec(memory_space=pl.ANY)
    phases = units // 2
    weight = pltpu.VMEM(w_query.shape, BF16)
    dma = pltpu.SemaphoreType.DMA
    return pl.pallas_call(
        functools.partial(kernel, n, ny),
        out_shape=jax.ShapeDtypeStruct(single.shape, BF16),
        in_specs=[vmem] * 4 + [smem] * 2 + [vmem] * 2 + [hbm] * 6,
        out_specs=vmem,
        scratch_shapes=[
            pltpu.VMEM((units, n, per, rows, width), BF16),
            pltpu.VMEM((units, per, rows, width), BF16),
            pltpu.VMEM((8, lanes), F32),
            pltpu.VMEM((n, 8, lanes), F32),
            pltpu.VMEM((heads, rows, width), BF16),
            pltpu.VMEM((heads, rows, keys), F32),
            pltpu.VMEM((samples, rows, width), BF16),
            pltpu.VMEM((samples, rows, width), F32),
            pltpu.VMEM((samples, rows, width), BF16),
            pltpu.VMEM((rows, samples, width), F32),
            pltpu.VMEM(pair.shape, BF16),
            weight, weight, weight, weight, weight,
            dma((6,)),
            dma((4, n)),
            dma((n,)),
            dma((units, n)),
            dma((phases,)),
            dma((phases, 2 * nz)),
            dma((phases, 2 * nz)),
            dma((phases, 2 * nz)),
            dma((phases, n)),
        ],
        compiler_params=pltpu.CompilerParams(
            collective_id=0, has_side_effects=True, vmem_limit_bytes=56 * 1024 * 1024
        ),
        cost_estimate=pl.CostEstimate(
            flops=7 * 10**9, bytes_accessed=10**7, transcendentals=10**6
        ),
    )(
        single, chain.reshape(1, rows), residue.reshape(1, rows), valid.reshape(1, rows),
        chain, residue, w_pair.T, rel_table.T, pair, w_query, w_key, w_value, w_gate, w_out,
    )


def solution(mesh):
    split = P(("groups", "tok"))
    rows = P(("groups", "tok"), None, None)
    return jax.shard_map(
        shards,
        mesh=mesh,
        in_specs=(rows, rows, split, split, split) + (P(),) * 7,
        out_specs=rows,
        check_vma=False,
    )
```
